32 devices in a mesh: groups: 2 (over y), row: 8 (over z, x), col: 2 (over core).
Axes of the slice: x: 2, y: 2, z: 4, core: 2. Of those that a mesh axis runs over, the one named last changes fastest.
Arguments:
- iterate: bfloat16 [16384, 3584], P(('groups', 'row'), 'col'), parts along dimension 0, may hold values from -6 to 6
Outputs:
- updated: bfloat16 [16384, 3584], P(('groups', 'row'), 'col'), parts along dimension 0
The draws below stay inside these ranges and needn't reach their ends.
There are 2 independent parts, one for each index of `groups`. The reference program is written for one: setup_inputs(seed, part) draws one part's arguments, and reference() takes and returns one part's arrays. A program takes and returns all parts, laid end to end along the dimension named above; each array names one. Nothing has to cross between parts.
All inputs are finite; a program needn't handle non-finite values.
Results may differ from the reference program's by a relative error of at most 0.0049.
Values may be sent and summed in bfloat16 or wider, within the bound.
No kernel may reach another device: no remote copies, remote signals or barrier semaphores. Data moves between devices by JAX's collectives and lax.ppermute only.
A program may use at most 128 MiB of HBM per device.

```python
import jax
import jax.numpy as jnp
from jax import lax

R = 8192
C = 3584


def steps_of(own_key, extent, pieces, least, top_value):
    def one(position, blocks):
        steps = jax.random.uniform(jax.random.fold_in(jax.random.fold_in(own_key, 6), position), (blocks,), jnp.float32, least / len(pieces), top_value / len(pieces))
        return jnp.repeat(jnp.exp(steps), extent[position] // blocks).reshape((-1,) + (1,) * (len(extent) - position - 1))

    level = one(*pieces[0])
    for cut in pieces[1:]:
        level = level * one(*cut)
    return level


def scatter_about(rng, shape, deviation, bound, split=(), dtype=jnp.bfloat16):
    values = jax.random.normal(rng, shape, jnp.float32) * deviation
    if len(split) > 0:
        values = steps_of(rng, shape, split, -0.22, 0.18) * values
    return jnp.clip(values, min=-bound, max=bound).astype(dtype)


def setup_inputs(seed: int = 0, part: int = 0) -> dict:
    key_of = jax.random.split(jax.random.key(seed), 2)
    own_keys = jax.random.split(jax.random.fold_in(key_of[1], part), 2)
    iterate = scatter_about(own_keys[0], (R, C), 0.6, 6.0, ((0, 8), (1, 2)))
    return {"iterate": iterate}


coef_linear = 3.4445
coef_cubic = -4.7750
coef_quintic = 2.0315


def reference(iterate):
    gram_full = lax.dot_general(iterate, iterate, (((0,), (0,)), ((), ())), preferred_element_type=jnp.float32) * (1.0 / R)
    gram_half = gram_full.astype(jnp.bfloat16)
    square = jnp.dot(gram_half, gram_half, preferred_element_type=jnp.float32)
    poly_matrix = (coef_cubic * gram_full + coef_quintic * square).astype(jnp.bfloat16)
    mixed = jnp.dot(iterate, poly_matrix, preferred_element_type=jnp.float32)
    return (coef_linear * iterate.astype(jnp.float32) + mixed).astype(jnp.bfloat16)
```

```python
import functools

import jax
import jax.numpy as jnp
from jax import lax
from jax.experimental import pallas as pl
from jax.experimental.pallas import tpu as pltpu
from jax.sharding import PartitionSpec as P

R = 8192

coef_linear = 3.4445
coef_cubic = -4.775
coef_quintic = 2.0315

PANEL = 256
RING_MOST = 16
F32 = jnp.float32
BF16 = jnp.bfloat16


def dot(a, b, ca, cb):
    return lax.dot_general(a, b, (((ca,), (cb,)), ((), ())), preferred_element_type=F32)


def packed_gram(own, panels, reach):
    width = reach * PANEL
    wrapped = jnp.concatenate([own, own[:, : width - PANEL]], 1)
    strips = []
    for i in range(panels):
        strips.append(dot(own[:, i * PANEL : (i + 1) * PANEL], wrapped[:, i * PANEL : i * PANEL + width], 0, 0))
    return jnp.concatenate(strips, 0) * (1.0 / R)


def finish_kernel(panels, reach, x_ref, d0_ref, c0_ref, d1_ref, c1_ref, o_ref, xe, ye, yf, cross):
    rows = x_ref.shape[0]
    half = panels * PANEL
    width = reach * PANEL
    part = c0_ref.shape[1]
    diag = (d0_ref, d1_ref)
    side = (c0_ref, c1_ref)

    def extend(dst, src):
        for h in range(2):
            dst[h, :, :half] = src[:, h * half : (h + 1) * half]
            dst[h, :, half:] = src[:, h * half : h * half + width - PANEL]

    def multiply(src, emit):
        for b in range(2):
            cross[:, b * part : (b + 1) * part] = dot(src[0, :, :half], side[b][...], 1, 0)

        @pl.loop(0, panels)
        def _(j):
            at = pl.multiple_of(j * PANEL, PANEL)
            here = pl.ds(at, PANEL)
            for h in range(2):
                total = dot(src[h, :, pl.ds(at, width)], diag[h][here, :], 1, 1)
                for d in range(1, reach):
                    other = pl.ds(pl.multiple_of(lax.rem(j + panels - d, panels) * PANEL, PANEL), PANEL)
                    total += dot(src[h, :, other], diag[h][other, d * PANEL : (d + 1) * PANEL], 1, 0)
                if h == 0:
                    for b in range(2):
                        total += dot(src[1, :, b * part : (b + 1) * part], side[b][here, :], 1, 1)
                else:
                    total += cross[:, here]
                emit(h, here, total)

    extend(xe, x_ref)

    def first(h, here, total):
        yf[h, :, here] = total
        ye[h, :, here] = total.astype(BF16)

    multiply(xe, first)
    for h in range(2):
        ye[h, :, half:] = ye[h, :, : width - PANEL]

    def second(h, here, total):
        linear = coef_linear * xe[h, :, here].astype(F32) + coef_cubic * yf[h, :, here]
        at = pl.multiple_of(h * half + here.start, PANEL)
        o_ref[:, pl.ds(at, PANEL)] = (linear + coef_quintic * total).astype(BF16)

    multiply(ye, second)


def finish(x, d0, c0, d1, c1, panels, reach):
    rows, cols = x.shape
    half = panels * PANEL
    extra = (reach - 1) * PANEL
    vmem = pl.BlockSpec(memory_space=pltpu.VMEM)
    return pl.pallas_call(
        functools.partial(finish_kernel, panels, reach),
        out_shape=jax.ShapeDtypeStruct((rows, cols), BF16),
        in_specs=[vmem] * 5,
        out_specs=vmem,
        scratch_shapes=[
            pltpu.VMEM((2, rows, half + extra), BF16),
            pltpu.VMEM((2, rows, half + extra), BF16),
            pltpu.VMEM((2, rows, half), F32),
            pltpu.VMEM((rows, half), F32),
        ],
        compiler_params=pltpu.CompilerParams(vmem_limit_bytes=60 * 2**20),
        cost_estimate=pl.CostEstimate(flops=4 * rows * cols * cols, bytes_accessed=2 * cols * cols, transcendentals=0),
    )(x, d0, c0, d1, c1)


def ring_exchange(blocks, count):
    order = list(range(0, count, 2)) + list(range(1, count, 2))[::-1]
    places = [order.index(r) for r in range(count)]
    place = jnp.array(places, jnp.int32)[lax.axis_index("row")]
    pairs = {}
    for turn in (1, -1):
        pairs[turn] = [(order[p], order[(p + turn) % count]) for p in range(count)]
    streams = []
    for block in blocks:
        step_rows = block.shape[0] // (2 * count)
        for turn in (1, -1):
            streams.append((block, turn, step_rows))

    def start_row(turn, step_rows, index):
        index = lax.rem(index + 4 * count, count)
        base = 0 if turn == 1 else count * step_rows
        return base + index * step_rows

    def own(stream, index):
        block, turn, step_rows = stream
        return lax.dynamic_slice_in_dim(block, start_row(turn, step_rows, index), step_rows, 0)

    held = [own(s, place - s[1]).astype(BF16) for s in streams]
    for step in range(count - 1):
        for k, s in enumerate(streams):
            turn = s[1]
            arrived = lax.ppermute(held[k], "row", pairs[turn])
            held[k] = (arrived.astype(F32) + own(s, place - turn * (step + 2))).astype(BF16)
    outs = [jnp.zeros(b.shape, BF16) for b in blocks]
    for step in range(count):
        for k, s in enumerate(streams):
            turn = s[1]
            at = start_row(turn, s[2], place - turn * step)
            outs[k // 2] = lax.dynamic_update_slice_in_dim(outs[k // 2], held[k], at, 0)
            if step < count - 1:
                held[k] = lax.ppermute(held[k], "row", pairs[turn])
    return outs


def plain_exchange(blocks):
    outs = []
    for block in blocks:
        mine = lax.psum_scatter(block.astype(BF16), "row", scatter_dimension=0, tiled=True)
        outs.append(lax.all_gather(mine, "row", axis=0, tiled=True))
    return outs


def body(iterate):
    rows, half = iterate.shape
    count = lax.axis_size("row")
    core = lax.axis_index("col")
    panels = half // PANEL
    reach = (panels + 1) // 2
    part = half // 2
    swap = [(0, 1), (1, 0)]
    first_core = core == 0

    other = lax.ppermute(iterate, "col", swap)
    diag_part = packed_gram(iterate, panels, reach)
    left = jnp.where(first_core, iterate, other)
    right = jnp.where(first_core, other, iterate)
    side_part = dot(left, lax.dynamic_slice_in_dim(right, core * part, part, 1), 0, 0) * (1.0 / R)

    if count <= RING_MOST:
        diag, side = ring_exchange([diag_part, side_part], count)
    else:
        diag, side = plain_exchange([diag_part, side_part])
    diag_other = lax.ppermute(diag, "col", swap)
    side_other = lax.ppermute(side, "col", swap)
    d0 = jnp.where(first_core, diag, diag_other)
    d1 = jnp.where(first_core, diag_other, diag)
    c0 = jnp.where(first_core, side, side_other)
    c1 = jnp.where(first_core, side_other, side)

    share = rows // 2
    at = core * share
    mine = jnp.concatenate(
        [lax.dynamic_slice_in_dim(left, at, share, 0), lax.dynamic_slice_in_dim(right, at, share, 0)], 1
    )
    done = finish(mine, d0, c0, d1, c1, panels, reach)
    keep = lax.dynamic_slice_in_dim(done, core * half, half, 1)
    send = lax.dynamic_slice_in_dim(done, (1 - core) * half, half, 1)
    got = lax.ppermute(send, "col", swap)
    return jnp.concatenate([jnp.where(first_core, keep, got), jnp.where(first_core, got, keep)], 0)


def solution(mesh):
    return jax.shard_map(
        body,
        mesh=mesh,
        in_specs=(P(("groups", "row"), "col"),),
        out_specs=P(("groups", "row"), "col"),
        check_vma=False,
    )
```

```python
import functools

import jax
import jax.numpy as jnp
from jax import lax
from jax.experimental import pallas as pl
from jax.experimental.pallas import tpu as pltpu
from jax.sharding import PartitionSpec as P

R = 8192

coef_linear = 3.4445
coef_cubic = -4.775
coef_quintic = 2.0315

PANEL = 256
RING_MOST = 16
F32 = jnp.float32
BF16 = jnp.bfloat16


def dot(a, b, ca, cb):
    return lax.dot_general(a, b, (((ca,), (cb,)), ((), ())), preferred_element_type=F32)


def diag_kernel(x_ref, o_ref, wide):
    half = x_ref.shape[1]
    width = o_ref.shape[1]
    wide[:, :half] = x_ref[...]
    wide[:, half:] = x_ref[:, : width - PANEL]
    for at in range(0, half, PANEL):
        strip = dot(x_ref[:, at : at + PANEL], wide[:, at : at + width], 0, 0)
        o_ref[at : at + PANEL, :] = (strip * (1.0 / R)).astype(BF16)


def diag_gram(x, width):
    rows, half = x.shape
    vmem = pl.BlockSpec(memory_space=pltpu.VMEM)
    return pl.pallas_call(
        diag_kernel,
        out_shape=jax.ShapeDtypeStruct((half, width), BF16),
        in_specs=[vmem],
        out_specs=vmem,
        scratch_shapes=[pltpu.VMEM((rows, half + width - PANEL), BF16)],
        compiler_params=pltpu.CompilerParams(vmem_limit_bytes=40 * 2**20),
        cost_estimate=pl.CostEstimate(flops=2 * rows * half * width, bytes_accessed=4 * rows * half, transcendentals=0),
    )(x)


def side_kernel(core_ref, own_ref, other_ref, o_ref):
    half = own_ref.shape[1]
    part = half // 2

    def go(left_ref, right_ref, start):
        for at in range(0, half, PANEL):
            strip = dot(left_ref[:, at : at + PANEL], right_ref[:, start : start + part], 0, 0)
            o_ref[at : at + PANEL, :] = (strip * (1.0 / R)).astype(BF16)

    @pl.when(core_ref[0] == 0)
    def _():
        go(own_ref, other_ref, 0)

    @pl.when(core_ref[0] == 1)
    def _():
        go(other_ref, own_ref, part)


def side_gram(core, own, other):
    rows, half = own.shape
    vmem = pl.BlockSpec(memory_space=pltpu.VMEM)
    return pl.pallas_call(
        side_kernel,
        out_shape=jax.ShapeDtypeStruct((half, half // 2), BF16),
        in_specs=[pl.BlockSpec(memory_space=pltpu.SMEM), vmem, vmem],
        out_specs=vmem,
        compiler_params=pltpu.CompilerParams(vmem_limit_bytes=40 * 2**20),
        cost_estimate=pl.CostEstimate(flops=rows * half * half, bytes_accessed=6 * rows * half, transcendentals=0),
    )(core.reshape(1), own, other)


def finish_kernel(panels, reach, part, pieces, place_ref, *refs):
    own_ref, other_ref = refs[:2]
    piece_refs = refs[2 : 2 + 2 * sum(pieces)]
    keep_ref, send_ref, xe, ye, yf, cross, diag, side, out, sems = refs[2 + 2 * sum(pieces) :]
    core = place_ref[0]
    rows = xe.shape[1]
    half = panels * PANEL
    width = reach * PANEL

    copies = []

    def bring(source, target):
        copy = pltpu.make_async_copy(source, target, sems.at[len(copies)])
        copy.start()
        copies.append(copy)

    mine = pl.ds(pl.multiple_of(core * rows, rows), rows)
    bring(own_ref.at[mine, :], xe.at[core, :, pl.ds(0, half)])
    bring(other_ref.at[mine, :], xe.at[1 - core, :, pl.ds(0, half)])
    at = 0
    for owner in (core, 1 - core):
        for k, store in enumerate((diag, side)):
            for m in range(pieces[k]):
                piece = piece_refs[at]
                start = place_ref[1 + m + (pieces[0] if k == 1 else 0)]
                start = pl.multiple_of(start, 16)
                bring(piece, store.at[owner, pl.ds(start, piece.shape[0]), :])
                at += 1
    for copy in copies:
        copy.wait()

    def multiply(src, emit):
        for b in range(2):
            cross[:, b * part : (b + 1) * part] = dot(src[0, :, :half], side[b], 1, 0)

        @pl.loop(0, panels)
        def _(j):
            at = pl.multiple_of(j * PANEL, PANEL)
            here = pl.ds(at, PANEL)
            for h in range(2):
                total = dot(src[h, :, pl.ds(at, width)], diag[h, here, :], 1, 1)
                for d in range(1, reach):
                    there = pl.ds(pl.multiple_of(lax.rem(j + panels - d, panels) * PANEL, PANEL), PANEL)
                    total += dot(src[h, :, there], diag[h, there, d * PANEL : (d + 1) * PANEL], 1, 0)
                if h == 0:
                    for b in range(2):
                        total += dot(src[1, :, b * part : (b + 1) * part], side[b, here, :], 1, 1)
                else:
                    total += cross[:, here]
                emit(h, here, total)

    for h in range(2):
        xe[h, :, half:] = xe[h, :, : width - PANEL]

    def first(h, here, total):
        yf[h, :, here] = total
        ye[h, :, here] = total.astype(BF16)

    multiply(xe, first)
    for h in range(2):
        ye[h, :, half:] = ye[h, :, : width - PANEL]

    def second(h, here, total):
        linear = coef_linear * xe[h, :, here].astype(F32) + coef_cubic * yf[h, :, here]
        out[h, :, here] = (linear + coef_quintic * total).astype(BF16)

    multiply(ye, second)
    last = [
        pltpu.make_async_copy(out.at[core], keep_ref, sems.at[0]),
        pltpu.make_async_copy(out.at[1 - core], send_ref, sems.at[1]),
    ]
    for copy in last:
        copy.start()
    for copy in last:
        copy.wait()


def finish(core, own, other, starts, mine, theirs, panels, reach):
    rows, half = own.shape
    share = rows // 2
    part = half // 2
    width = reach * PANEL
    pieces = tuple(len(p) for p in mine)
    operands = [own, other, *mine[0], *mine[1], *theirs[0], *theirs[1]]
    place = jnp.stack([core, *starts]).astype(jnp.int32)
    anywhere = pl.BlockSpec(memory_space=pl.ANY)
    return pl.pallas_call(
        functools.partial(finish_kernel, panels, reach, part, pieces),
        out_shape=[jax.ShapeDtypeStruct((share, half), BF16)] * 2,
        in_specs=[pl.BlockSpec(memory_space=pltpu.SMEM)] + [anywhere] * len(operands),
        out_specs=[anywhere] * 2,
        scratch_shapes=[
            pltpu.VMEM((2, share, half + width - PANEL), BF16),
            pltpu.VMEM((2, share, half + width - PANEL), BF16),
            pltpu.VMEM((2, share, half), F32),
            pltpu.VMEM((share, half), F32),
            pltpu.VMEM((2, half, width), BF16),
            pltpu.VMEM((2, half, part), BF16),
            pltpu.VMEM((2, share, half), BF16),
            pltpu.SemaphoreType.DMA((len(operands),)),
        ],
        compiler_params=pltpu.CompilerParams(vmem_limit_bytes=56 * 2**20),
        cost_estimate=pl.CostEstimate(flops=16 * share * half * half, bytes_accessed=8 * half * half, transcendentals=0),
    )(place, *operands)


def join_kernel(core_ref, keep_ref, got_ref, o_ref):
    core = core_ref[0]
    rows = keep_ref.shape[0]
    o_ref[pl.ds(pl.multiple_of(core * rows, rows), rows), :] = keep_ref[...]
    o_ref[pl.ds(pl.multiple_of((1 - core) * rows, rows), rows), :] = got_ref[...]


def join(core, keep, got):
    rows, cols = keep.shape
    vmem = pl.BlockSpec(memory_space=pltpu.VMEM)
    return pl.pallas_call(
        join_kernel,
        out_shape=jax.ShapeDtypeStruct((2 * rows, cols), BF16),
        in_specs=[pl.BlockSpec(memory_space=pltpu.SMEM), vmem, vmem],
        out_specs=vmem,
    )(core.reshape(1), keep, got)


def ring_exchange(blocks):
    count = lax.axis_size("row")
    order = list(range(0, count, 2)) + list(range(1, count, 2))[::-1]
    places = [order.index(r) for r in range(count)]
    place = jnp.array(places, jnp.int32)[lax.axis_index("row")]
    far = count // 2
    turns = (1, -1)
    pairs = {t: [(order[p], order[(p + t) % count]) for p in range(count)] for t in turns}
    sizes = [b.shape[0] // count for b in blocks]

    def row_of(k, distance):
        return lax.rem(place + distance + count, count) * sizes[k]

    def own(k, distance):
        return lax.dynamic_slice_in_dim(blocks[k], row_of(k, distance), sizes[k], 0)

    def half_of(value, turn):
        middle = value.shape[0] // 2
        return value[:middle] if turn == 1 else value[middle:]

    def add(a, b):
        return (a.astype(F32) + b.astype(F32)).astype(BF16)

    parts = range(len(blocks))
    held = {(k, t): half_of(own(k, far), t).astype(BF16) for k in parts for t in turns}
    for distance in range(far - 1, -1, -1):
        for k in parts:
            arrived = {t: lax.ppermute(held[k, t], "row", pairs[t]) for t in turns}
            if distance == 0:
                total = own(k, 0).astype(F32)
                total = total + arrived[1].astype(F32) + arrived[-1].astype(F32)
                held[k, 1] = held[k, -1] = total.astype(BF16)
                continue
            for t in turns:
                mine = own(k, t * distance)
                if distance == far - 1:
                    middle = mine.shape[0] // 2
                    if t == 1:
                        held[k, t] = jnp.concatenate([add(mine[:middle], arrived[t]), mine[middle:].astype(BF16)], 0)
                    else:
                        held[k, t] = jnp.concatenate([mine[:middle].astype(BF16), add(mine[middle:], arrived[t])], 0)
                else:
                    held[k, t] = add(mine, arrived[t])
    pieces = [[held[k, 1]] for k in parts]
    starts = [[row_of(k, 0)] for k in parts]
    for distance in range(1, far + 1):
        for k in parts:
            for t in turns:
                sent = held[k, t] if distance < far else half_of(held[k, t], t)
                held[k, t] = lax.ppermute(sent, "row", pairs[t])
                at = row_of(k, -t * distance)
                if distance == far and t == -1:
                    at = at + sizes[k] // 2
                pieces[k].append(held[k, t])
                starts[k].append(at)
    return pieces, starts[0] + starts[1]


def plain_exchange(blocks):
    pieces = []
    for block in blocks:
        mine = lax.psum_scatter(block, "row", scatter_dimension=0, tiled=True)
        pieces.append([lax.all_gather(mine, "row", axis=0, tiled=True)])
    return pieces, [jnp.int32(0)] * len(blocks)


def body(iterate):
    half = iterate.shape[1]
    count = lax.axis_size("row")
    core = lax.axis_index("col")
    panels = half // PANEL
    reach = (panels + 1) // 2
    swap = [(0, 1), (1, 0)]

    other = lax.ppermute(iterate, "col", swap)
    diag_part = diag_gram(iterate, reach * PANEL)
    side_part = side_gram(core, iterate, other)
    diag_part, side_part = lax.optimization_barrier((diag_part, side_part))
    exchange = ring_exchange if count <= RING_MOST else plain_exchange
    mine, starts = exchange([diag_part, side_part])
    theirs = [[lax.ppermute(piece, "col", swap) for piece in kind] for kind in mine]
    keep, send = finish(core, iterate, other, starts, mine, theirs, panels, reach)
    return join(core, keep, lax.ppermute(send, "col", swap))


def solution(mesh):
    return jax.shard_map(
        body,
        mesh=mesh,
        in_specs=(P(("groups", "row"), "col"),),
        out_specs=P(("groups", "row"), "col"),
        check_vma=False,
    )
```

```python
import functools

import jax
import jax.numpy as jnp
from jax import lax
from jax.experimental import pallas as pl
from jax.experimental.pallas import tpu as pltpu
from jax.sharding import PartitionSpec as P

R = 8192

coef_linear = 3.4445
coef_cubic = -4.775
coef_quintic = 2.0315

PANEL = 256
RING_MOST = 16
STEP_BYTES = 20 * 2**20
STEP_FLOPS = 8 * 10**9
F32 = jnp.float32
BF16 = jnp.bfloat16


def dot(a, b, ca, cb):
    return lax.dot_general(a, b, (((ca,), (cb,)), ((), ())), preferred_element_type=F32)


def diag_kernel(x_ref, o_ref, wide):
    half = x_ref.shape[1]
    width = o_ref.shape[1]
    wide[:, :half] = x_ref[...]
    wide[:, half:] = x_ref[:, : width - PANEL]
    for at in range(0, half, PANEL):
        strip = dot(x_ref[:, at : at + PANEL], wide[:, at : at + width], 0, 0)
        o_ref[at : at + PANEL, :] = (strip * (1.0 / R)).astype(BF16)


def diag_gram(x, width):
    rows, half = x.shape
    vmem = pl.BlockSpec(memory_space=pltpu.VMEM)
    return pl.pallas_call(
        diag_kernel,
        out_shape=jax.ShapeDtypeStruct((half, width), BF16),
        in_specs=[vmem],
        out_specs=vmem,
        scratch_shapes=[pltpu.VMEM((rows, half + width - PANEL), BF16)],
        compiler_params=pltpu.CompilerParams(vmem_limit_bytes=40 * 2**20),
        cost_estimate=pl.CostEstimate(flops=2 * rows * half * width, bytes_accessed=4 * rows * half, transcendentals=0),
    )(x)


def side_kernel(core_ref, own_ref, other_ref, o_ref):
    half = own_ref.shape[1]
    part = half // 2

    def go(left_ref, right_ref, start):
        for at in range(0, half, PANEL):
            strip = dot(left_ref[:, at : at + PANEL], right_ref[:, start : start + part], 0, 0)
            o_ref[at : at + PANEL, :] = (strip * (1.0 / R)).astype(BF16)

    @pl.when(core_ref[0] == 0)
    def _():
        go(own_ref, other_ref, 0)

    @pl.when(core_ref[0] == 1)
    def _():
        go(other_ref, own_ref, part)


def side_gram(core, own, other):
    rows, half = own.shape
    vmem = pl.BlockSpec(memory_space=pltpu.VMEM)
    return pl.pallas_call(
        side_kernel,
        out_shape=jax.ShapeDtypeStruct((half, half // 2), BF16),
        in_specs=[pl.BlockSpec(memory_space=pltpu.SMEM), vmem, vmem],
        out_specs=vmem,
        compiler_params=pltpu.CompilerParams(vmem_limit_bytes=40 * 2**20),
        cost_estimate=pl.CostEstimate(flops=STEP_FLOPS, bytes_accessed=6 * rows * half, transcendentals=0),
    )(core.reshape(1), own, other)


def finish_kernel(panels, reach, part, pieces, place_ref, *refs):
    own_ref, other_ref = refs[:2]
    piece_refs = refs[2 : 2 + 2 * sum(pieces)]
    keep_ref, send_ref, xe, ye, yf, diag, side, out, sems = refs[2 + 2 * sum(pieces) :]
    core = place_ref[0]
    rows = xe.shape[1]
    half = panels * PANEL
    width = reach * PANEL

    copies = []

    def bring(source, target):
        copy = pltpu.make_async_copy(source, target, sems.at[len(copies)])
        copy.start()
        copies.append(copy)

    mine = pl.ds(pl.multiple_of(core * rows, rows), rows)
    bring(own_ref.at[mine, :], xe.at[core, :, pl.ds(0, half)])
    bring(other_ref.at[mine, :], xe.at[1 - core, :, pl.ds(0, half)])
    at = 0
    for owner in (core, 1 - core):
        for k, store in enumerate((diag, side)):
            for m in range(pieces[k]):
                piece = piece_refs[at]
                start = place_ref[1 + m + (pieces[0] if k == 1 else 0)]
                start = pl.multiple_of(start, 16)
                bring(piece, store.at[owner, pl.ds(start, piece.shape[0]), :])
                at += 1
    early = 2 + pieces[0]
    late = early + pieces[1]
    diag_copies = copies[:early] + copies[late : late + pieces[0]]
    side_copies = copies[early:late] + copies[late + pieces[0] :]

    def around(src, h, j):
        at = pl.multiple_of(j * PANEL, PANEL)
        total = dot(src[h, :, pl.ds(at, width)], diag[h, pl.ds(at, PANEL), :], 1, 1)
        for d in range(1, reach):
            there = pl.ds(pl.multiple_of(lax.rem(j + panels - d, panels) * PANEL, PANEL), PANEL)
            total += dot(src[h, :, there], diag[h, there, d * PANEL : (d + 1) * PANEL], 1, 0)
        return total

    def across(src, h, b):
        if h == 1:
            return dot(src[0, :, :half], side[b], 1, 0)
        here = slice(b * part, (b + 1) * part)
        return sum(dot(src[1, :, e * part : (e + 1) * part], side[e, here, :], 1, 1) for e in range(2))

    for copy in diag_copies:
        copy.wait()
    for h in range(2):
        xe[h, :, half:] = xe[h, :, : width - PANEL]

    @pl.loop(0, panels)
    def _(j):
        here = pl.ds(pl.multiple_of(j * PANEL, PANEL), PANEL)
        for h in range(2):
            yf[h, :, here] = around(xe, h, j)

    for copy in side_copies:
        copy.wait()
    for h in range(2):
        for b in range(2):
            here = slice(b * part, (b + 1) * part)
            total = yf[h, :, here] + across(xe, h, b)
            ye[h, :, here] = total.astype(BF16)
            yf[h, :, here] = coef_linear * xe[h, :, here].astype(F32) + coef_cubic * total
    for h in range(2):
        ye[h, :, half:] = ye[h, :, : width - PANEL]

    for h in range(2):
        for b in range(2):
            here = slice(b * part, (b + 1) * part)
            yf[h, :, here] += coef_quintic * across(ye, h, b)

    @pl.loop(0, panels)
    def _(j):
        here = pl.ds(pl.multiple_of(j * PANEL, PANEL), PANEL)
        for h in range(2):
            out[h, :, here] = (yf[h, :, here] + coef_quintic * around(ye, h, j)).astype(BF16)

    last = [
        pltpu.make_async_copy(out.at[core], keep_ref.at[mine, :], sems.at[0]),
        pltpu.make_async_copy(out.at[1 - core], send_ref, sems.at[1]),
    ]
    for copy in last:
        copy.start()
    for copy in last:
        copy.wait()


def finish(core, own, other, starts, mine, theirs, panels, reach):
    rows, half = own.shape
    share = rows // 2
    part = half // 2
    width = reach * PANEL
    pieces = tuple(len(p) for p in mine)
    operands = [own, other, *mine[0], *mine[1], *theirs[0], *theirs[1]]
    place = jnp.stack([core, *starts]).astype(jnp.int32)
    anywhere = pl.BlockSpec(memory_space=pl.ANY)
    return pl.pallas_call(
        functools.partial(finish_kernel, panels, reach, part, pieces),
        out_shape=[jax.ShapeDtypeStruct((n, half), BF16) for n in (rows, share)],
        in_specs=[pl.BlockSpec(memory_space=pltpu.SMEM)] + [anywhere] * len(operands),
        out_specs=[anywhere] * 2,
        scratch_shapes=[
            pltpu.VMEM((2, share, half + width - PANEL), BF16),
            pltpu.VMEM((2, share, half + width - PANEL), BF16),
            pltpu.VMEM((2, share, half), F32),
            pltpu.VMEM((2, half, width), BF16),
            pltpu.VMEM((2, half, part), BF16),
            pltpu.VMEM((2, share, half), BF16),
            pltpu.SemaphoreType.DMA((len(operands),)),
        ],
        compiler_params=pltpu.CompilerParams(vmem_limit_bytes=56 * 2**20),
        cost_estimate=pl.CostEstimate(flops=16 * share * half * half, bytes_accessed=8 * half * half, transcendentals=0),
    )(place, *operands)


def add_kernel(kind, place_ref, forth_ref, back_ref, block_ref, *refs):
    out_refs, (own, sems) = refs[-4:-2] if kind != "last" else refs[-3:-2], refs[-2:]
    size = out_refs[0].shape[0]
    middle = size // 2
    copies = []
    for i in range(len(out_refs)):
        start = pl.multiple_of(place_ref[i], 16)
        copies.append(pltpu.make_async_copy(block_ref.at[pl.ds(start, size), :], own.at[i], sems.at[i]))
    for copy in copies:
        copy.start()
    for copy in copies:
        copy.wait()

    if kind == "last":
        total = own[0].astype(F32) + forth_ref[...].astype(F32) + back_ref[...].astype(F32)
        out_refs[0][...] = total.astype(BF16)
    elif kind == "middle":
        out_refs[0][...] = own[0] + forth_ref[...]
        out_refs[1][...] = own[1] + back_ref[...]
    else:
        out_refs[0][:middle] = own[0, :middle] + forth_ref[...]
        out_refs[0][middle:] = own[0, middle:]
        out_refs[1][:middle] = own[1, :middle]
        out_refs[1][middle:] = own[1, middle:] + back_ref[...]


def add_step(kind, size, starts, forth, back, block, after):
    outs = 1 if kind == "last" else 2
    cols = block.shape[1]
    vmem = pl.BlockSpec(memory_space=pltpu.VMEM)
    anywhere = pl.BlockSpec(memory_space=pl.ANY)
    return pl.pallas_call(
        functools.partial(add_kernel, kind),
        out_shape=[jax.ShapeDtypeStruct((size, cols), BF16)] * outs,
        in_specs=[pl.BlockSpec(memory_space=pltpu.SMEM), vmem, vmem] + [anywhere] * (1 + len(after)),
        out_specs=[vmem] * outs,
        scratch_shapes=[pltpu.VMEM((outs, size, cols), BF16), pltpu.SemaphoreType.DMA((outs,))],
        cost_estimate=pl.CostEstimate(flops=STEP_FLOPS // 2, bytes_accessed=8 * size * cols, transcendentals=0),
    )(jnp.stack(starts).astype(jnp.int32), forth, back, block, *after)


def gate(values, after):
    anywhere = pl.BlockSpec(memory_space=pl.ANY)
    return pl.pallas_call(
        lambda *refs: None,
        out_shape=[jax.ShapeDtypeStruct(v.shape, v.dtype) for v in values],
        in_specs=[anywhere] * (len(values) + len(after)),
        out_specs=[anywhere] * len(values),
        input_output_aliases={i: i for i in range(len(values))},
        cost_estimate=pl.CostEstimate(flops=STEP_FLOPS, bytes_accessed=STEP_BYTES, transcendentals=0),
    )(*values, *after)


def ring_exchange(blocks):
    count = lax.axis_size("row")
    order = list(range(0, count, 2)) + list(range(1, count, 2))[::-1]
    places = [order.index(r) for r in range(count)]
    place = jnp.array(places, jnp.int32)[lax.axis_index("row")]
    far = count // 2
    turns = (1, -1)
    pairs = {t: [(order[p], order[(p + t) % count]) for p in range(count)] for t in turns}
    sizes = [b.shape[0] // count for b in blocks]
    parts = range(len(blocks))

    def row_of(k, distance):
        return lax.rem(place + distance + count, count) * sizes[k]

    def half_of(value, turn):
        middle = value.shape[0] // 2
        return value[:middle] if turn == 1 else value[middle:]

    def pass_on(values):
        return [lax.ppermute(v, "row", pairs[t]) for t, v in zip(turns, values, strict=True)]

    held = []
    for k in parts:
        whole = lax.dynamic_slice_in_dim(blocks[k], row_of(k, far), sizes[k], 0)
        held.append([half_of(whole, t) for t in turns])
    after = blocks[1:]
    for distance in range(far - 1, -1, -1):
        kind = "last" if distance == 0 else "first" if distance == far - 1 else "middle"
        for k in parts:
            forth, back = pass_on(held[k])
            starts = [row_of(k, distance), row_of(k, -distance)][: 1 if distance == 0 else 2]
            held[k] = add_step(kind, sizes[k], starts, forth, back, blocks[k], after)
            after = [held[k][0]]
    pieces = [[held[k][0]] for k in parts]
    starts = [[row_of(k, 0)] for k in parts]
    held = [[h[0], h[0]] for h in held]
    for distance in range(1, far + 1):
        for k in parts:
            if distance == far:
                held[k] = [half_of(h, t) for t, h in zip(turns, held[k], strict=True)]
            held[k] = gate(pass_on(held[k]), after)
            after = [held[k][0]]
            pieces[k] += held[k]
            ends = [row_of(k, -distance), row_of(k, distance)]
            if distance == far:
                ends[1] = ends[1] + sizes[k] // 2
            starts[k] += ends
    return pieces, starts[0] + starts[1]


def plain_exchange(blocks):
    pieces = []
    for block in blocks:
        mine = lax.psum_scatter(block, "row", scatter_dimension=0, tiled=True)
        pieces.append([lax.all_gather(mine, "row", axis=0, tiled=True)])
    return pieces, [jnp.int32(0)] * len(blocks)


def body(iterate):
    half = iterate.shape[1]
    count = lax.axis_size("row")
    core = lax.axis_index("col")
    panels = half // PANEL
    reach = (panels + 1) // 2
    swap = [(0, 1), (1, 0)]

    other = lax.ppermute(iterate, "col", swap)
    diag_part = diag_gram(iterate, reach * PANEL)
    side_part = side_gram(core, iterate, other)
    exchange = ring_exchange if count <= RING_MOST else plain_exchange
    mine, starts = exchange([diag_part, side_part])
    theirs = [[lax.ppermute(piece, "col", swap) for piece in kind] for kind in mine]
    keep, send = finish(core, iterate, other, starts, mine, theirs, panels, reach)
    got = lax.ppermute(send, "col", swap)
    return lax.dynamic_update_slice_in_dim(keep, got, (1 - core) * got.shape[0], 0)


def solution(mesh):
    return jax.shard_map(
        body,
        mesh=mesh,
        in_specs=(P(("groups", "row"), "col"),),
        out_specs=P(("groups", "row"), "col"),
        check_vma=False,
    )
```

```python
import functools

import jax
import jax.numpy as jnp
from jax import lax
from jax.experimental import pallas as pl
from jax.experimental.pallas import tpu as pltpu
from jax.sharding import PartitionSpec as P

R = 8192

coef_linear = 3.4445
coef_cubic = -4.775
coef_quintic = 2.0315

PANEL = 256
RING_MOST = 16
STEP_BYTES = 20 * 2**20
STEP_FLOPS = 8 * 10**9
F32 = jnp.float32
BF16 = jnp.bfloat16


def dot(a, b, ca, cb):
    return lax.dot_general(a, b, (((ca,), (cb,)), ((), ())), preferred_element_type=F32)


def diag_kernel(x_ref, o_ref, wide):
    half = x_ref.shape[1]
    width = o_ref.shape[1]
    wide[:, :half] = x_ref[...]
    wide[:, half:] = x_ref[:, : width - PANEL]
    for at in range(0, half, PANEL):
        strip = dot(x_ref[:, at : at + PANEL], wide[:, at : at + width], 0, 0)
        o_ref[at : at + PANEL, :] = (strip * (1.0 / R)).astype(BF16)


def diag_gram(x, width):
    rows, half = x.shape
    vmem = pl.BlockSpec(memory_space=pltpu.VMEM)
    return pl.pallas_call(
        diag_kernel,
        out_shape=jax.ShapeDtypeStruct((half, width), BF16),
        in_specs=[vmem],
        out_specs=vmem,
        scratch_shapes=[pltpu.VMEM((rows, half + width - PANEL), BF16)],
        compiler_params=pltpu.CompilerParams(vmem_limit_bytes=40 * 2**20),
        cost_estimate=pl.CostEstimate(flops=2 * rows * half * width, bytes_accessed=4 * rows * half, transcendentals=0),
    )(x)


def side_kernel(core_ref, own_ref, other_ref, o_ref):
    half = own_ref.shape[1]
    part = half // 2

    def go(left_ref, right_ref, start):
        for at in range(0, half, PANEL):
            strip = dot(left_ref[:, at : at + PANEL], right_ref[:, start : start + part], 0, 0)
            o_ref[at : at + PANEL, :] = (strip * (1.0 / R)).astype(BF16)

    @pl.when(core_ref[0] == 0)
    def _():
        go(own_ref, other_ref, 0)

    @pl.when(core_ref[0] == 1)
    def _():
        go(other_ref, own_ref, part)


def side_gram(core, own, other):
    rows, half = own.shape
    vmem = pl.BlockSpec(memory_space=pltpu.VMEM)
    return pl.pallas_call(
        side_kernel,
        out_shape=jax.ShapeDtypeStruct((half, half // 2), BF16),
        in_specs=[pl.BlockSpec(memory_space=pltpu.SMEM), vmem, vmem],
        out_specs=vmem,
        compiler_params=pltpu.CompilerParams(vmem_limit_bytes=40 * 2**20),
        cost_estimate=pl.CostEstimate(flops=STEP_FLOPS, bytes_accessed=6 * rows * half, transcendentals=0),
    )(core.reshape(1), own, other)


def finish_kernel(panels, reach, part, pieces, place_ref, *refs):
    own_ref, other_ref = refs[:2]
    piece_refs = refs[2 : 2 + 2 * sum(pieces)]
    keep_ref, send_ref, xe, ye, yf, diag, side, out, sems = refs[2 + 2 * sum(pieces) :]
    core = place_ref[0]
    rows = xe.shape[1]
    half = panels * PANEL
    width = reach * PANEL

    copies = []

    def bring(source, target):
        copy = pltpu.make_async_copy(source, target, sems.at[len(copies)])
        copy.start()
        copies.append(copy)

    mine = pl.ds(pl.multiple_of(core * rows, rows), rows)
    bring(own_ref.at[mine, :], xe.at[core, :, pl.ds(0, half)])
    bring(other_ref.at[mine, :], xe.at[1 - core, :, pl.ds(0, half)])
    at = 0
    for owner in (core, 1 - core):
        for k, store in enumerate((diag, side)):
            for m in range(pieces[k]):
                piece = piece_refs[at]
                start = place_ref[1 + m + (pieces[0] if k == 1 else 0)]
                start = pl.multiple_of(start, 16)
                bring(piece, store.at[owner, pl.ds(start, piece.shape[0]), :])
                at += 1
    early = 2 + pieces[0]
    late = early + pieces[1]
    diag_copies = copies[:early] + copies[late : late + pieces[0]]
    side_copies = copies[early:late] + copies[late + pieces[0] :]

    def around(src, h, j):
        at = pl.multiple_of(j * PANEL, PANEL)
        total = dot(src[h, :, pl.ds(at, width)], diag[h, pl.ds(at, PANEL), :], 1, 1)
        for d in range(1, reach):
            there = pl.ds(pl.multiple_of(lax.rem(j + panels - d, panels) * PANEL, PANEL), PANEL)
            total += dot(src[h, :, there], diag[h, there, d * PANEL : (d + 1) * PANEL], 1, 0)
        return total

    def across(src, h, b):
        if h == 1:
            return dot(src[0, :, :half], side[b], 1, 0)
        here = slice(b * part, (b + 1) * part)
        return sum(dot(src[1, :, e * part : (e + 1) * part], side[e, here, :], 1, 1) for e in range(2))

    for copy in diag_copies:
        copy.wait()
    for h in range(2):
        xe[h, :, half:] = xe[h, :, : width - PANEL]

    @pl.loop(0, panels, unroll=True)
    def _(j):
        here = pl.ds(pl.multiple_of(j * PANEL, PANEL), PANEL)
        for h in range(2):
            yf[h, :, here] = around(xe, h, j)

    for copy in side_copies:
        copy.wait()
    for h in range(2):
        for b in range(2):
            here = slice(b * part, (b + 1) * part)
            total = yf[h, :, here] + across(xe, h, b)
            ye[h, :, here] = total.astype(BF16)
            yf[h, :, here] = coef_linear * xe[h, :, here].astype(F32) + coef_cubic * total
    for h in range(2):
        ye[h, :, half:] = ye[h, :, : width - PANEL]

    for h in range(2):
        for b in range(2):
            here = slice(b * part, (b + 1) * part)
            yf[h, :, here] += coef_quintic * across(ye, h, b)

    @pl.loop(0, panels, unroll=True)
    def _(j):
        here = pl.ds(pl.multiple_of(j * PANEL, PANEL), PANEL)
        for h in range(2):
            out[h, :, here] = (yf[h, :, here] + coef_quintic * around(ye, h, j)).astype(BF16)

    last = [
        pltpu.make_async_copy(out.at[core], keep_ref.at[mine, :], sems.at[0]),
        pltpu.make_async_copy(out.at[1 - core], send_ref, sems.at[1]),
    ]
    for copy in last:
        copy.start()
    for copy in last:
        copy.wait()


def finish(core, own, other, starts, mine, theirs, panels, reach):
    rows, half = own.shape
    share = rows // 2
    part = half // 2
    width = reach * PANEL
    pieces = tuple(len(p) for p in mine)
    operands = [own, other, *mine[0], *mine[1], *theirs[0], *theirs[1]]
    place = jnp.stack([core, *starts]).astype(jnp.int32)
    anywhere = pl.BlockSpec(memory_space=pl.ANY)
    return pl.pallas_call(
        functools.partial(finish_kernel, panels, reach, part, pieces),
        out_shape=[jax.ShapeDtypeStruct((n, half), BF16) for n in (rows, share)],
        in_specs=[pl.BlockSpec(memory_space=pltpu.SMEM)] + [anywhere] * len(operands),
        out_specs=[anywhere] * 2,
        scratch_shapes=[
            pltpu.VMEM((2, share, half + width - PANEL), BF16),
            pltpu.VMEM((2, share, half + width - PANEL), BF16),
            pltpu.VMEM((2, share, half), F32),
            pltpu.VMEM((2, half, width), BF16),
            pltpu.VMEM((2, half, part), BF16),
            pltpu.VMEM((2, share, half), BF16),
            pltpu.SemaphoreType.DMA((len(operands),)),
        ],
        compiler_params=pltpu.CompilerParams(vmem_limit_bytes=56 * 2**20),
        cost_estimate=pl.CostEstimate(flops=16 * share * half * half, bytes_accessed=8 * half * half, transcendentals=0),
    )(place, *operands)


def add_kernel(kind, place_ref, forth_ref, back_ref, block_ref, *refs):
    out_refs, (own, sems) = refs[-4:-2] if kind != "last" else refs[-3:-2], refs[-2:]
    size = out_refs[0].shape[0]
    middle = size // 2
    copies = []
    for i in range(len(out_refs)):
        start = pl.multiple_of(place_ref[i], 16)
        copies.append(pltpu.make_async_copy(block_ref.at[pl.ds(start, size), :], own.at[i], sems.at[i]))
    for copy in copies:
        copy.start()
    for copy in copies:
        copy.wait()

    if kind == "last":
        total = own[0].astype(F32) + forth_ref[...].astype(F32) + back_ref[...].astype(F32)
        out_refs[0][...] = total.astype(BF16)
    elif kind == "middle":
        out_refs[0][...] = own[0] + forth_ref[...]
        out_refs[1][...] = own[1] + back_ref[...]
    else:
        out_refs[0][:middle] = own[0, :middle] + forth_ref[...]
        out_refs[0][middle:] = own[0, middle:]
        out_refs[1][:middle] = own[1, :middle]
        out_refs[1][middle:] = own[1, middle:] + back_ref[...]


def add_step(kind, size, starts, forth, back, block, after):
    outs = 1 if kind == "last" else 2
    cols = block.shape[1]
    vmem = pl.BlockSpec(memory_space=pltpu.VMEM)
    anywhere = pl.BlockSpec(memory_space=pl.ANY)
    return pl.pallas_call(
        functools.partial(add_kernel, kind),
        out_shape=[jax.ShapeDtypeStruct((size, cols), BF16)] * outs,
        in_specs=[pl.BlockSpec(memory_space=pltpu.SMEM), vmem, vmem] + [anywhere] * (1 + len(after)),
        out_specs=[vmem] * outs,
        scratch_shapes=[pltpu.VMEM((outs, size, cols), BF16), pltpu.SemaphoreType.DMA((outs,))],
        compiler_params=pltpu.CompilerParams(vmem_limit_bytes=8 * 2**20),
        cost_estimate=pl.CostEstimate(flops=STEP_FLOPS, bytes_accessed=8 * size * cols, transcendentals=0),
    )(jnp.stack(starts).astype(jnp.int32), forth, back, block, *after)


def gate(values, after):
    anywhere = pl.BlockSpec(memory_space=pl.ANY)
    return pl.pallas_call(
        lambda *refs: None,
        out_shape=[jax.ShapeDtypeStruct(v.shape, v.dtype) for v in values],
        in_specs=[anywhere] * (len(values) + len(after)),
        out_specs=[anywhere] * len(values),
        input_output_aliases={i: i for i in range(len(values))},
        compiler_params=pltpu.CompilerParams(vmem_limit_bytes=2**20),
        cost_estimate=pl.CostEstimate(flops=STEP_FLOPS, bytes_accessed=STEP_BYTES, transcendentals=0),
    )(*values, *after)


def ring_exchange(blocks):
    count = lax.axis_size("row")
    order = list(range(0, count, 2)) + list(range(1, count, 2))[::-1]
    row = lax.axis_index("row")
    place = jnp.where(row % 2 == 0, row // 2, count - 1 - row // 2)
    far = count // 2
    turns = (1, -1)
    pairs = {t: [(order[p], order[(p + t) % count]) for p in range(count)] for t in turns}
    sizes = [b.shape[0] // count for b in blocks]
    parts = range(len(blocks))

    def row_of(k, distance):
        return lax.rem(place + distance + count, count) * sizes[k]

    def half_of(value, turn):
        middle = value.shape[0] // 2
        return value[:middle] if turn == 1 else value[middle:]

    def pass_on(values):
        values = lax.optimization_barrier(tuple(values))
        return [lax.ppermute(v, "row", pairs[t]) for t, v in zip(turns, values, strict=True)]

    held = []
    for k in parts:
        whole = lax.dynamic_slice_in_dim(blocks[k], row_of(k, far), sizes[k], 0)
        held.append([half_of(whole, t) for t in turns])
    after = blocks[1:]
    for distance in range(far - 1, -1, -1):
        kind = "last" if distance == 0 else "first" if distance == far - 1 else "middle"
        for k in parts:
            forth, back = pass_on(held[k])
            starts = [row_of(k, distance), row_of(k, -distance)][: 1 if distance == 0 else 2]
            held[k] = add_step(kind, sizes[k], starts, forth, back, blocks[k], after)
            after = [held[k][0]]
    pieces = [[held[k][0]] for k in parts]
    starts = [[row_of(k, 0)] for k in parts]
    held = [[h[0], h[0]] for h in held]
    for distance in range(1, far + 1):
        for k in parts:
            if distance == far:
                held[k] = [half_of(h, t) for t, h in zip(turns, held[k], strict=True)]
            held[k] = gate(pass_on(held[k]), after)
            after = [held[k][0]]
            pieces[k] += held[k]
            ends = [row_of(k, -distance), row_of(k, distance)]
            if distance == far:
                ends[1] = ends[1] + sizes[k] // 2
            starts[k] += ends
    return pieces, starts[0] + starts[1]


def plain_exchange(blocks):
    pieces = []
    for block in blocks:
        mine = lax.psum_scatter(block, "row", scatter_dimension=0, tiled=True)
        pieces.append([lax.all_gather(mine, "row", axis=0, tiled=True)])
    return pieces, [jnp.int32(0)] * len(blocks)


def body(iterate):
    half = iterate.shape[1]
    count = lax.axis_size("row")
    core = lax.axis_index("col")
    panels = half // PANEL
    reach = (panels + 1) // 2
    swap = [(0, 1), (1, 0)]

    other = lax.ppermute(iterate, "col", swap)
    diag_part = diag_gram(iterate, reach * PANEL)
    side_part = side_gram(core, iterate, other)
    exchange = ring_exchange if count <= RING_MOST else plain_exchange
    mine, starts = exchange([diag_part, side_part])
    theirs = [[lax.ppermute(piece, "col", swap) for piece in kind] for kind in mine]
    keep, send = finish(core, iterate, other, starts, mine, theirs, panels, reach)
    got = lax.ppermute(send, "col", swap)
    return lax.dynamic_update_slice_in_dim(keep, got, (1 - core) * got.shape[0], 0)


def solution(mesh):
    return jax.shard_map(
        body,
        mesh=mesh,
        in_specs=(P(("groups", "row"), "col"),),
        out_specs=P(("groups", "row"), "col"),
        check_vma=False,
    )
```

```python
import functools

import jax
import jax.numpy as jnp
from jax import lax
from jax.experimental import pallas as pl
from jax.experimental.pallas import tpu as pltpu
from jax.sharding import PartitionSpec as P

R = 8192

coef_linear = 3.4445
coef_cubic = -4.775
coef_quintic = 2.0315

PANEL = 256
RING_MOST = 16
STEP_BYTES = 20 * 2**20
STEP_FLOPS = 8 * 10**9
F32 = jnp.float32
BF16 = jnp.bfloat16


def dot(a, b, ca, cb):
    return lax.dot_general(a, b, (((ca,), (cb,)), ((), ())), preferred_element_type=F32)


def emit_chunk(start, o_ref, chunk_refs):
    for i, ref in enumerate(chunk_refs):
        size = ref.shape[0]
        ref[...] = o_ref[pl.ds(pl.multiple_of(start + i * size, 16), size), :]


def diag_kernel(place_ref, x_ref, o_ref, *refs):
    chunk_refs, wide = refs[:-1], refs[-1]
    half = x_ref.shape[1]
    width = o_ref.shape[1]
    wide[:, :half] = x_ref[...]
    wide[:, half:] = x_ref[:, : width - PANEL]
    for at in range(0, half, PANEL):
        strip = dot(x_ref[:, at : at + PANEL], wide[:, at : at + width], 0, 0)
        o_ref[at : at + PANEL, :] = (strip * (1.0 / R)).astype(BF16)
    emit_chunk(place_ref[0], o_ref, chunk_refs)


def gram_outs(half, width, size):
    return [jax.ShapeDtypeStruct((n, width), BF16) for n in ([half] if size is None else [half, size // 2, size // 2])]


def diag_gram(x, width, start, size):
    rows, half = x.shape
    outs = gram_outs(half, width, size)
    vmem = pl.BlockSpec(memory_space=pltpu.VMEM)
    return pl.pallas_call(
        diag_kernel,
        out_shape=outs,
        in_specs=[pl.BlockSpec(memory_space=pltpu.SMEM), vmem],
        out_specs=[vmem] * len(outs),
        scratch_shapes=[pltpu.VMEM((rows, half + width - PANEL), BF16)],
        compiler_params=pltpu.CompilerParams(vmem_limit_bytes=40 * 2**20),
        cost_estimate=pl.CostEstimate(flops=2 * rows * half * width, bytes_accessed=4 * rows * half, transcendentals=0),
    )(start.reshape(1), x)


def side_kernel(outs, place_ref, own_ref, other_ref, *refs):
    o_ref, chunk_refs = refs[-outs], refs[len(refs) - outs + 1 :]
    half = own_ref.shape[1]
    part = half // 2

    def go(left_ref, right_ref, start):
        for at in range(0, half, PANEL):
            strip = dot(left_ref[:, at : at + PANEL], right_ref[:, start : start + part], 0, 0)
            o_ref[at : at + PANEL, :] = (strip * (1.0 / R)).astype(BF16)

    @pl.when(place_ref[1] == 0)
    def _():
        go(own_ref, other_ref, 0)

    @pl.when(place_ref[1] == 1)
    def _():
        go(other_ref, own_ref, part)

    emit_chunk(place_ref[0], o_ref, chunk_refs)


def side_gram(core, own, other, start, size):
    rows, half = own.shape
    outs = gram_outs(half, half // 2, size)
    vmem = pl.BlockSpec(memory_space=pltpu.VMEM)
    return pl.pallas_call(
        functools.partial(side_kernel, len(outs)),
        out_shape=outs,
        in_specs=[pl.BlockSpec(memory_space=pltpu.SMEM), vmem, vmem],
        out_specs=[vmem] * len(outs),
        compiler_params=pltpu.CompilerParams(vmem_limit_bytes=40 * 2**20),
        cost_estimate=pl.CostEstimate(flops=STEP_FLOPS, bytes_accessed=6 * rows * half, transcendentals=0),
    )(jnp.stack([start, core]), own, other)


def finish_kernel(panels, reach, part, pieces, place_ref, *refs):
    own_ref, other_ref = refs[:2]
    piece_refs = refs[2 : 2 + 2 * sum(pieces)]
    keep_ref, send_ref, xe, ye, yf, diag, side, out, sems = refs[2 + 2 * sum(pieces) :]
    core = place_ref[0]
    rows = xe.shape[1]
    half = panels * PANEL
    width = reach * PANEL

    copies = []

    def bring(source, target):
        copy = pltpu.make_async_copy(source, target, sems.at[len(copies)])
        copy.start()
        copies.append(copy)

    mine = pl.ds(pl.multiple_of(core * rows, rows), rows)
    bring(own_ref.at[mine, :], xe.at[core, :, pl.ds(0, half)])
    bring(other_ref.at[mine, :], xe.at[1 - core, :, pl.ds(0, half)])
    at = 0
    for owner in (core, 1 - core):
        for k, store in enumerate((diag, side)):
            for m in range(pieces[k]):
                piece = piece_refs[at]
                start = place_ref[1 + m + (pieces[0] if k == 1 else 0)]
                start = pl.multiple_of(start, 16)
                bring(piece, store.at[owner, pl.ds(start, piece.shape[0]), :])
                at += 1
    early = 2 + pieces[0]
    late = early + pieces[1]
    diag_copies = copies[:early] + copies[late : late + pieces[0]]
    side_copies = copies[early:late] + copies[late + pieces[0] :]

    def around(src, h, j):
        at = pl.multiple_of(j * PANEL, PANEL)
        total = dot(src[h, :, pl.ds(at, width)], diag[h, pl.ds(at, PANEL), :], 1, 1)
        for d in range(1, reach):
            there = pl.ds(pl.multiple_of(lax.rem(j + panels - d, panels) * PANEL, PANEL), PANEL)
            total += dot(src[h, :, there], diag[h, there, d * PANEL : (d + 1) * PANEL], 1, 0)
        return total

    def across(src, h, b):
        if h == 1:
            return dot(src[0, :, :half], side[b], 1, 0)
        here = slice(b * part, (b + 1) * part)
        return sum(dot(src[1, :, e * part : (e + 1) * part], side[e, here, :], 1, 1) for e in range(2))

    for copy in diag_copies:
        copy.wait()
    for h in range(2):
        xe[h, :, half:] = xe[h, :, : width - PANEL]

    @pl.loop(0, panels)
    def _(j):
        here = pl.ds(pl.multiple_of(j * PANEL, PANEL), PANEL)
        for h in range(2):
            yf[h, :, here] = around(xe, h, j)

    for copy in side_copies:
        copy.wait()
    for h in range(2):
        for b in range(2):
            here = slice(b * part, (b + 1) * part)
            total = yf[h, :, here] + across(xe, h, b)
            ye[h, :, here] = total.astype(BF16)
            yf[h, :, here] = coef_linear * xe[h, :, here].astype(F32) + coef_cubic * total
    for h in range(2):
        ye[h, :, half:] = ye[h, :, : width - PANEL]

    for h in range(2):
        for b in range(2):
            here = slice(b * part, (b + 1) * part)
            yf[h, :, here] += coef_quintic * across(ye, h, b)

    @pl.loop(0, panels)
    def _(j):
        here = pl.ds(pl.multiple_of(j * PANEL, PANEL), PANEL)
        for h in range(2):
            out[h, :, here] = (yf[h, :, here] + coef_quintic * around(ye, h, j)).astype(BF16)

    last = [
        pltpu.make_async_copy(out.at[core], keep_ref.at[mine, :], sems.at[0]),
        pltpu.make_async_copy(out.at[1 - core], send_ref, sems.at[1]),
    ]
    for copy in last:
        copy.start()
    for copy in last:
        copy.wait()


def finish(core, own, other, starts, mine, theirs, panels, reach):
    rows, half = own.shape
    share = rows // 2
    part = half // 2
    width = reach * PANEL
    pieces = tuple(len(p) for p in mine)
    operands = [own, other, *mine[0], *mine[1], *theirs[0], *theirs[1]]
    place = jnp.stack([core, *starts]).astype(jnp.int32)
    anywhere = pl.BlockSpec(memory_space=pl.ANY)
    return pl.pallas_call(
        functools.partial(finish_kernel, panels, reach, part, pieces),
        out_shape=[jax.ShapeDtypeStruct((n, half), BF16) for n in (rows, share)],
        in_specs=[pl.BlockSpec(memory_space=pltpu.SMEM)] + [anywhere] * len(operands),
        out_specs=[anywhere] * 2,
        scratch_shapes=[
            pltpu.VMEM((2, share, half + width - PANEL), BF16),
            pltpu.VMEM((2, share, half + width - PANEL), BF16),
            pltpu.VMEM((2, share, half), F32),
            pltpu.VMEM((2, half, width), BF16),
            pltpu.VMEM((2, half, part), BF16),
            pltpu.VMEM((2, share, half), BF16),
            pltpu.SemaphoreType.DMA((len(operands),)),
        ],
        compiler_params=pltpu.CompilerParams(vmem_limit_bytes=56 * 2**20),
        cost_estimate=pl.CostEstimate(flops=16 * share * half * half, bytes_accessed=8 * half * half, transcendentals=0),
    )(place, *operands)


def add_kernel(kind, place_ref, forth_ref, back_ref, block_ref, *refs):
    out_refs, (own, sems) = refs[-4:-2] if kind != "last" else refs[-3:-2], refs[-2:]
    size = out_refs[0].shape[0]
    middle = size // 2
    copies = []
    for i in range(len(out_refs)):
        start = pl.multiple_of(place_ref[i], 16)
        copies.append(pltpu.make_async_copy(block_ref.at[pl.ds(start, size), :], own.at[i], sems.at[i]))
    for copy in copies:
        copy.start()
    for copy in copies:
        copy.wait()

    if kind == "last":
        total = own[0].astype(F32) + forth_ref[...].astype(F32) + back_ref[...].astype(F32)
        out_refs[0][...] = total.astype(BF16)
    elif kind == "middle":
        out_refs[0][...] = own[0] + forth_ref[...]
        out_refs[1][...] = own[1] + back_ref[...]
    else:
        out_refs[0][:middle] = own[0, :middle] + forth_ref[...]
        out_refs[0][middle:] = own[0, middle:]
        out_refs[1][:middle] = own[1, :middle]
        out_refs[1][middle:] = own[1, middle:] + back_ref[...]


def add_step(kind, size, starts, forth, back, block, after):
    outs = 1 if kind == "last" else 2
    cols = block.shape[1]
    vmem = pl.BlockSpec(memory_space=pltpu.VMEM)
    anywhere = pl.BlockSpec(memory_space=pl.ANY)
    return pl.pallas_call(
        functools.partial(add_kernel, kind),
        out_shape=[jax.ShapeDtypeStruct((size, cols), BF16)] * outs,
        in_specs=[pl.BlockSpec(memory_space=pltpu.SMEM), vmem, vmem] + [anywhere] * (1 + len(after)),
        out_specs=[vmem] * outs,
        scratch_shapes=[pltpu.VMEM((outs, size, cols), BF16), pltpu.SemaphoreType.DMA((outs,))],
        compiler_params=pltpu.CompilerParams(vmem_limit_bytes=8 * 2**20),
        cost_estimate=pl.CostEstimate(flops=STEP_FLOPS, bytes_accessed=8 * size * cols, transcendentals=0),
    )(jnp.stack(starts).astype(jnp.int32), forth, back, block, *after)


def gate(values, after):
    anywhere = pl.BlockSpec(memory_space=pl.ANY)
    return pl.pallas_call(
        lambda *refs: None,
        out_shape=[jax.ShapeDtypeStruct(v.shape, v.dtype) for v in values],
        in_specs=[anywhere] * (len(values) + len(after)),
        out_specs=[anywhere] * len(values),
        input_output_aliases={i: i for i in range(len(values))},
        compiler_params=pltpu.CompilerParams(vmem_limit_bytes=2**20),
        cost_estimate=pl.CostEstimate(flops=STEP_FLOPS, bytes_accessed=STEP_BYTES, transcendentals=0),
    )(*values, *after)


def ring_exchange(half, makers):
    count = lax.axis_size("row")
    order = list(range(0, count, 2)) + list(range(1, count, 2))[::-1]
    row = lax.axis_index("row")
    place = jnp.where(row % 2 == 0, row // 2, count - 1 - row // 2)
    far = count // 2
    turns = (1, -1)
    pairs = {t: [(order[p], order[(p + t) % count]) for p in range(count)] for t in turns}
    size = half // count
    parts = range(len(makers))

    def row_of(distance):
        return lax.rem(place + distance + count, count) * size

    def half_of(value, turn):
        middle = value.shape[0] // 2
        return value[:middle] if turn == 1 else value[middle:]

    def pass_on(values):
        values = lax.optimization_barrier(tuple(values))
        return [lax.ppermute(v, "row", pairs[t]) for t, v in zip(turns, values, strict=True)]

    blocks, held = [], []
    for make in makers:
        block, *chunk = make(row_of(far), size)
        blocks.append(block)
        held.append(chunk)
    after = blocks[1:]
    for distance in range(far - 1, -1, -1):
        kind = "last" if distance == 0 else "first" if distance == far - 1 else "middle"
        for k in parts:
            forth, back = pass_on(held[k])
            starts = [row_of(distance), row_of(-distance)][: 1 if distance == 0 else 2]
            held[k] = add_step(kind, size, starts, forth, back, blocks[k], after)
            after = [held[k][0]]
    pieces = [[held[k][0]] for k in parts]
    starts = [[row_of(0)] for k in parts]
    held = [[h[0], h[0]] for h in held]
    for distance in range(1, far + 1):
        for k in parts:
            if distance == far:
                held[k] = [half_of(h, t) for t, h in zip(turns, held[k], strict=True)]
            held[k] = gate(pass_on(held[k]), after)
            after = [held[k][0]]
            pieces[k] += held[k]
            ends = [row_of(-distance), row_of(distance)]
            if distance == far:
                ends[1] = ends[1] + size // 2
            starts[k] += ends
    return pieces, starts[0] + starts[1]


def plain_exchange(half, makers):
    pieces = []
    for make in makers:
        (block,) = make(jnp.int32(0), None)
        mine = lax.psum_scatter(block, "row", scatter_dimension=0, tiled=True)
        pieces.append([lax.all_gather(mine, "row", axis=0, tiled=True)])
    return pieces, [jnp.int32(0)] * len(makers)


def body(iterate):
    half = iterate.shape[1]
    count = lax.axis_size("row")
    core = lax.axis_index("col")
    panels = half // PANEL
    reach = (panels + 1) // 2
    swap = [(0, 1), (1, 0)]

    other = lax.ppermute(iterate, "col", swap)
    makers = [
        lambda start, size: diag_gram(iterate, reach * PANEL, start, size),
        lambda start, size: side_gram(core, iterate, other, start, size),
    ]
    exchange = ring_exchange if count <= RING_MOST else plain_exchange
    mine, starts = exchange(half, makers)
    theirs = [[lax.ppermute(piece, "col", swap) for piece in kind] for kind in mine]
    keep, send = finish(core, iterate, other, starts, mine, theirs, panels, reach)
    got = lax.ppermute(send, "col", swap)
    return lax.dynamic_update_slice_in_dim(keep, got, (1 - core) * got.shape[0], 0)


def solution(mesh):
    return jax.shard_map(
        body,
        mesh=mesh,
        in_specs=(P(("groups", "row"), "col"),),
        out_specs=P(("groups", "row"), "col"),
        check_vma=False,
    )
```

```python
import functools

import jax
import jax.numpy as jnp
from jax import lax
from jax.experimental import pallas as pl
from jax.experimental.pallas import tpu as pltpu
from jax.sharding import PartitionSpec as P

R = 8192

coef_linear = 3.4445
coef_cubic = -4.775
coef_quintic = 2.0315

PANEL = 256
RING_MOST = 16
STEP_BYTES = 20 * 2**20
SUM_FLOPS = 8 * 10**9
GATE_FLOPS = 3 * 10**9
F32 = jnp.float32
BF16 = jnp.bfloat16


def dot(a, b, ca, cb):
    return lax.dot_general(a, b, (((ca,), (cb,)), ((), ())), preferred_element_type=F32)


def emit_chunk(start, o_ref, chunk_refs):
    for i, ref in enumerate(chunk_refs):
        size = ref.shape[0]
        ref[...] = o_ref[pl.ds(pl.multiple_of(start + i * size, 16), size), :]


def diag_kernel(place_ref, x_ref, o_ref, *refs):
    chunk_refs, wide = refs[:-1], refs[-1]
    half = x_ref.shape[1]
    width = o_ref.shape[1]
    wide[:, :half] = x_ref[...]
    wide[:, half:] = x_ref[:, : width - PANEL]
    for at in range(0, half, PANEL):
        strip = dot(x_ref[:, at : at + PANEL], wide[:, at : at + width], 0, 0)
        o_ref[at : at + PANEL, :] = (strip * (1.0 / R)).astype(BF16)
    emit_chunk(place_ref[0], o_ref, chunk_refs)


def gram_outs(half, width, size):
    return [jax.ShapeDtypeStruct((n, width), BF16) for n in ([half] if size is None else [half, size // 2, size // 2])]


def diag_gram(x, width, start, size):
    rows, half = x.shape
    outs = gram_outs(half, width, size)
    vmem = pl.BlockSpec(memory_space=pltpu.VMEM)
    return pl.pallas_call(
        diag_kernel,
        out_shape=outs,
        in_specs=[pl.BlockSpec(memory_space=pltpu.SMEM), vmem],
        out_specs=[vmem] * len(outs),
        scratch_shapes=[pltpu.VMEM((rows, half + width - PANEL), BF16)],
        compiler_params=pltpu.CompilerParams(vmem_limit_bytes=40 * 2**20),
        cost_estimate=pl.CostEstimate(flops=2 * rows * half * width, bytes_accessed=4 * rows * half, transcendentals=0),
    )(start.reshape(1), x)


def side_kernel(outs, place_ref, own_ref, other_ref, *refs):
    o_ref, chunk_refs = refs[-outs], refs[len(refs) - outs + 1 :]
    half = own_ref.shape[1]
    part = half // 2

    def go(left_ref, right_ref, start):
        for at in range(0, half, PANEL):
            strip = dot(left_ref[:, at : at + PANEL], right_ref[:, start : start + part], 0, 0)
            o_ref[at : at + PANEL, :] = (strip * (1.0 / R)).astype(BF16)

    @pl.when(place_ref[1] == 0)
    def _():
        go(own_ref, other_ref, 0)

    @pl.when(place_ref[1] == 1)
    def _():
        go(other_ref, own_ref, part)

    emit_chunk(place_ref[0], o_ref, chunk_refs)


def side_gram(core, own, other, start, size):
    rows, half = own.shape
    outs = gram_outs(half, half // 2, size)
    vmem = pl.BlockSpec(memory_space=pltpu.VMEM)
    return pl.pallas_call(
        functools.partial(side_kernel, len(outs)),
        out_shape=outs,
        in_specs=[pl.BlockSpec(memory_space=pltpu.SMEM), vmem, vmem],
        out_specs=[vmem] * len(outs),
        compiler_params=pltpu.CompilerParams(vmem_limit_bytes=40 * 2**20),
        cost_estimate=pl.CostEstimate(flops=SUM_FLOPS, bytes_accessed=6 * rows * half, transcendentals=0),
    )(jnp.stack([start, core]), own, other)


def finish_kernel(panels, reach, part, pieces, place_ref, *refs):
    own_ref, other_ref = refs[:2]
    piece_refs = refs[2 : 2 + 2 * sum(pieces)]
    keep_ref, send_ref, xe, ye, yf, diag, side, out, sems = refs[2 + 2 * sum(pieces) :]
    core = place_ref[0]
    rows = xe.shape[1]
    half = panels * PANEL
    width = reach * PANEL

    copies = []

    def bring(source, target):
        copy = pltpu.make_async_copy(source, target, sems.at[len(copies)])
        copy.start()
        copies.append(copy)

    mine = pl.ds(pl.multiple_of(core * rows, rows), rows)
    bring(own_ref.at[mine, :], xe.at[core, :, pl.ds(0, half)])
    bring(other_ref.at[mine, :], xe.at[1 - core, :, pl.ds(0, half)])
    at = 0
    for owner in (core, 1 - core):
        for k, store in enumerate((diag, side)):
            for m in range(pieces[k]):
                piece = piece_refs[at]
                start = place_ref[1 + m + (pieces[0] if k == 1 else 0)]
                start = pl.multiple_of(start, 16)
                bring(piece, store.at[owner, pl.ds(start, piece.shape[0]), :])
                at += 1
    early = 2 + pieces[0]
    late = early + pieces[1]
    diag_copies = copies[:early] + copies[late : late + pieces[0]]
    side_copies = copies[early:late] + copies[late + pieces[0] :]

    def around(src, h, j):
        at = pl.multiple_of(j * PANEL, PANEL)
        total = dot(src[h, :, pl.ds(at, width)], diag[h, pl.ds(at, PANEL), :], 1, 1)
        for d in range(1, reach):
            there = pl.ds(pl.multiple_of(lax.rem(j + panels - d, panels) * PANEL, PANEL), PANEL)
            total += dot(src[h, :, there], diag[h, there, d * PANEL : (d + 1) * PANEL], 1, 0)
        return total

    def across(src, h, b):
        if h == 1:
            return dot(src[0, :, :half], side[b], 1, 0)
        here = slice(b * part, (b + 1) * part)
        return sum(dot(src[1, :, e * part : (e + 1) * part], side[e, here, :], 1, 1) for e in range(2))

    for copy in diag_copies:
        copy.wait()
    for h in range(2):
        xe[h, :, half:] = xe[h, :, : width - PANEL]

    @pl.loop(0, panels)
    def _(j):
        here = pl.ds(pl.multiple_of(j * PANEL, PANEL), PANEL)
        for h in range(2):
            yf[h, :, here] = around(xe, h, j)

    for copy in side_copies:
        copy.wait()
    for h in range(2):
        for b in range(2):
            here = slice(b * part, (b + 1) * part)
            total = yf[h, :, here] + across(xe, h, b)
            ye[h, :, here] = total.astype(BF16)
            yf[h, :, here] = coef_linear * xe[h, :, here].astype(F32) + coef_cubic * total
    for h in range(2):
        ye[h, :, half:] = ye[h, :, : width - PANEL]

    for h in range(2):
        for b in range(2):
            here = slice(b * part, (b + 1) * part)
            yf[h, :, here] += coef_quintic * across(ye, h, b)

    @pl.loop(0, panels)
    def _(j):
        here = pl.ds(pl.multiple_of(j * PANEL, PANEL), PANEL)
        for h in range(2):
            out[h, :, here] = (yf[h, :, here] + coef_quintic * around(ye, h, j)).astype(BF16)

    last = [
        pltpu.make_async_copy(out.at[core], keep_ref.at[mine, :], sems.at[0]),
        pltpu.make_async_copy(out.at[1 - core], send_ref, sems.at[1]),
    ]
    for copy in last:
        copy.start()
    for copy in last:
        copy.wait()


def finish(core, own, other, starts, mine, theirs, panels, reach):
    rows, half = own.shape
    share = rows // 2
    part = half // 2
    width = reach * PANEL
    pieces = tuple(len(p) for p in mine)
    operands = [own, other, *mine[0], *mine[1], *theirs[0], *theirs[1]]
    place = jnp.stack([core, *starts]).astype(jnp.int32)
    anywhere = pl.BlockSpec(memory_space=pl.ANY)
    return pl.pallas_call(
        functools.partial(finish_kernel, panels, reach, part, pieces),
        out_shape=[jax.ShapeDtypeStruct((n, half), BF16) for n in (rows, share)],
        in_specs=[pl.BlockSpec(memory_space=pltpu.SMEM)] + [anywhere] * len(operands),
        out_specs=[anywhere] * 2,
        scratch_shapes=[
            pltpu.VMEM((2, share, half + width - PANEL), BF16),
            pltpu.VMEM((2, share, half + width - PANEL), BF16),
            pltpu.VMEM((2, share, half), F32),
            pltpu.VMEM((2, half, width), BF16),
            pltpu.VMEM((2, half, part), BF16),
            pltpu.VMEM((2, share, half), BF16),
            pltpu.SemaphoreType.DMA((len(operands),)),
        ],
        compiler_params=pltpu.CompilerParams(vmem_limit_bytes=56 * 2**20),
        cost_estimate=pl.CostEstimate(flops=16 * share * half * half, bytes_accessed=8 * half * half, transcendentals=0),
    )(place, *operands)


def add_kernel(kind, place_ref, forth_ref, back_ref, block_ref, *refs):
    out_refs, (own, sems) = refs[-4:-2] if kind != "last" else refs[-3:-2], refs[-2:]
    size = out_refs[0].shape[0]
    middle = size // 2
    copies = []
    for i in range(len(out_refs)):
        start = pl.multiple_of(place_ref[i], 16)
        copies.append(pltpu.make_async_copy(block_ref.at[pl.ds(start, size), :], own.at[i], sems.at[i]))
    for copy in copies:
        copy.start()
    for copy in copies:
        copy.wait()

    if kind == "last":
        total = own[0].astype(F32) + forth_ref[...].astype(F32) + back_ref[...].astype(F32)
        out_refs[0][...] = total.astype(BF16)
    elif kind == "middle":
        out_refs[0][...] = own[0] + forth_ref[...]
        out_refs[1][...] = own[1] + back_ref[...]
    else:
        out_refs[0][:middle] = own[0, :middle] + forth_ref[...]
        out_refs[0][middle:] = own[0, middle:]
        out_refs[1][:middle] = own[1, :middle]
        out_refs[1][middle:] = own[1, middle:] + back_ref[...]


def add_step(kind, size, starts, forth, back, block, after):
    outs = 1 if kind == "last" else 2
    cols = block.shape[1]
    vmem = pl.BlockSpec(memory_space=pltpu.VMEM)
    anywhere = pl.BlockSpec(memory_space=pl.ANY)
    return pl.pallas_call(
        functools.partial(add_kernel, kind),
        out_shape=[jax.ShapeDtypeStruct((size, cols), BF16)] * outs,
        in_specs=[pl.BlockSpec(memory_space=pltpu.SMEM), vmem, vmem] + [anywhere] * (1 + len(after)),
        out_specs=[vmem] * outs,
        scratch_shapes=[pltpu.VMEM((outs, size, cols), BF16), pltpu.SemaphoreType.DMA((outs,))],
        compiler_params=pltpu.CompilerParams(vmem_limit_bytes=8 * 2**20),
        cost_estimate=pl.CostEstimate(flops=SUM_FLOPS, bytes_accessed=8 * size * cols, transcendentals=0),
    )(jnp.stack(starts).astype(jnp.int32), forth, back, block, *after)


def gate(values, after):
    anywhere = pl.BlockSpec(memory_space=pl.ANY)
    return pl.pallas_call(
        lambda *refs: None,
        out_shape=[jax.ShapeDtypeStruct(v.shape, v.dtype) for v in values],
        in_specs=[anywhere] * (len(values) + len(after)),
        out_specs=[anywhere] * len(values),
        input_output_aliases={i: i for i in range(len(values))},
        compiler_params=pltpu.CompilerParams(vmem_limit_bytes=2**20),
        cost_estimate=pl.CostEstimate(flops=GATE_FLOPS, bytes_accessed=STEP_BYTES, transcendentals=0),
    )(*values, *after)


def ring_exchange(half, makers):
    count = lax.axis_size("row")
    order = list(range(0, count, 2)) + list(range(1, count, 2))[::-1]
    row = lax.axis_index("row")
    place = jnp.where(row % 2 == 0, row // 2, count - 1 - row // 2)
    far = count // 2
    turns = (1, -1)
    pairs = {t: [(order[p], order[(p + t) % count]) for p in range(count)] for t in turns}
    size = half // count
    parts = range(len(makers))

    def row_of(distance):
        return lax.rem(place + distance + count, count) * size

    def half_of(value, turn):
        middle = value.shape[0] // 2
        return value[:middle] if turn == 1 else value[middle:]

    def pass_on(values):
        values = lax.optimization_barrier(tuple(values))
        return [lax.ppermute(v, "row", pairs[t]) for t, v in zip(turns, values, strict=True)]

    blocks, held = [], []
    for make in makers:
        block, *chunk = make(row_of(far), size)
        blocks.append(block)
        held.append(chunk)
    after = blocks[1:]
    for distance in range(far - 1, -1, -1):
        kind = "last" if distance == 0 else "first" if distance == far - 1 else "middle"
        for k in parts:
            forth, back = pass_on(held[k])
            starts = [row_of(distance), row_of(-distance)][: 1 if distance == 0 else 2]
            held[k] = add_step(kind, size, starts, forth, back, blocks[k], after)
            after = [held[k][0]]
    pieces = [[held[k][0]] for k in parts]
    starts = [[row_of(0)] for k in parts]
    held = [[h[0], h[0]] for h in held]
    for distance in range(1, far + 1):
        for k in parts:
            if distance == far:
                held[k] = [half_of(h, t) for t, h in zip(turns, held[k], strict=True)]
            held[k] = gate(pass_on(held[k]), after)
            after = [held[k][0]]
            pieces[k] += held[k]
            ends = [row_of(-distance), row_of(distance)]
            if distance == far:
                ends[1] = ends[1] + size // 2
            starts[k] += ends
    return pieces, starts[0] + starts[1]


def plain_exchange(half, makers):
    pieces = []
    for make in makers:
        (block,) = make(jnp.int32(0), None)
        mine = lax.psum_scatter(block, "row", scatter_dimension=0, tiled=True)
        pieces.append([lax.all_gather(mine, "row", axis=0, tiled=True)])
    return pieces, [jnp.int32(0)] * len(makers)


def body(iterate):
    half = iterate.shape[1]
    count = lax.axis_size("row")
    core = lax.axis_index("col")
    panels = half // PANEL
    reach = (panels + 1) // 2
    swap = [(0, 1), (1, 0)]

    other = lax.ppermute(iterate, "col", swap)
    makers = [
        lambda start, size: diag_gram(iterate, reach * PANEL, start, size),
        lambda start, size: side_gram(core, iterate, other, start, size),
    ]
    exchange = ring_exchange if count <= RING_MOST else plain_exchange
    mine, starts = exchange(half, makers)
    theirs = [[lax.ppermute(piece, "col", swap) for piece in kind] for kind in mine]
    keep, send = finish(core, iterate, other, starts, mine, theirs, panels, reach)
    got = lax.ppermute(send, "col", swap)
    return lax.dynamic_update_slice_in_dim(keep, got, (1 - core) * got.shape[0], 0)


def solution(mesh):
    return jax.shard_map(
        body,
        mesh=mesh,
        in_specs=(P(("groups", "row"), "col"),),
        out_specs=P(("groups", "row"), "col"),
        check_vma=False,
    )
```
